32 devices in a mesh: grp: 2 (over y), op: 4 (over x, core), sec: 4 (over z).
Axes of the slice: x: 2, y: 2, z: 4, core: 2. Of those that a mesh axis runs over, the one named last changes fastest.
Arguments:
- psi: bfloat16 [32, 2, 256, 256], P(('grp', 'sec')), parts along dimension 0, may hold values from -6 to 6
- left_env: bfloat16 [8, 32, 256, 256], P('op', ('grp', 'sec')), parts along dimension 1, may hold values from -0.375 to 0.375
- right_env: bfloat16 [8, 32, 256, 256], P('op', ('grp', 'sec')), parts along dimension 1, may hold values from -0.125 to 0.125
- sector_dims: int32 [2, 32], P(None, 'grp'), parts along dimension 1, may hold values from 64 to 256, as said below
- right_place: int32 [32], P('grp'), parts along dimension 0, may hold values from 0 to 15, as said below
Outputs:
- sigma: bfloat16 [32, 2, 256, 256], P(('grp', 'sec'), None, 'op'), parts along dimension 0
The draws below stay inside these ranges and needn't reach their ends.
There are 2 independent parts, one for each index of `grp`. The reference program is written for one: setup_inputs(seed, part) draws one part's arguments, and reference() takes and returns one part's arrays. A program takes and returns all parts, laid end to end along the dimension named above; each array names one. Nothing has to cross between parts.
Inputs may be any that keep to these rules, and one draw needn't show every extreme that they name: `sector_dims`: in each row one block has exactly 256. `right_place`: A permutation of the blocks; the 4 blocks i * 4 to i * 4 + 3 go to positions of 4 different ranges j * 4 to j * 4 + 3.
All inputs are finite; a program needn't handle non-finite values.
Results may differ from the reference program's by a relative error of at most 0.0049.
Values may be sent and summed in bfloat16 or wider, within the bound.
No kernel may reach another device: no remote copies, remote signals or barrier semaphores. Data moves between devices by JAX's collectives and lax.ppermute only.
A program may use at most 64 MiB of HBM per device.

```python
import jax
import jax.numpy as jnp
from jax import lax

P_SIZE = 256
V = 2
NB_DEV = 4
NB = 16
K = 8


def draw_sector_dims(key, part):
    key = jax.random.fold_in(key, 11)
    first, second = jax.random.split(key)
    dims = jax.random.randint(first, (2, NB), P_SIZE // 4, P_SIZE + 1)
    where_full = jax.random.randint(second, (2,), 0, NB)
    dims = dims.at[0, where_full[0]].set(P_SIZE)
    dims = dims.at[1, where_full[1]].set(P_SIZE)
    return dims.astype(jnp.int32)


def draw_right_place(key, part):
    key = jax.random.fold_in(key, 23)
    owners = NB // NB_DEV
    keys = jax.random.split(key, 4)
    first_perm = jax.random.permutation(keys[0], owners)
    second_perm = jax.random.permutation(keys[1], owners)
    offsets = jax.random.permutation(keys[2], owners)[:NB_DEV]
    turns = jax.random.randint(keys[3], (owners,), 0, NB_DEV)
    blocks = jnp.arange(NB, dtype=jnp.int32)
    source = blocks // NB_DEV
    within = blocks % NB_DEV
    target = second_perm[(first_perm[source] + offsets[within]) % owners]
    slot = (within + turns[target]) % NB_DEV
    return (target * NB_DEV + slot).astype(jnp.int32)


def levels(own_key, shape, cuts, least, largest):
    level = 1.0
    for dim, blocks in cuts:
        draws = jax.random.uniform(jax.random.fold_in(jax.random.fold_in(own_key, 6), dim), (blocks,), jnp.float32, least / len(cuts), largest / len(cuts))
        level = level * jnp.repeat(jnp.exp(draws), shape[dim] // blocks).reshape((-1,) + (1,) * (len(shape) - 1 - dim))
    return level


def centred(key, extent, scale, limit, pieces=(), kind=jnp.bfloat16):
    array = scale * jax.random.normal(key, extent, jnp.float32)
    if pieces:
        array = array * levels(key, extent, pieces, -0.22, 0.18)
    return jnp.clip(array, -limit, limit).astype(kind)


def setup_inputs(seed: int = 0, part: int = 0) -> dict:
    key_list = jax.random.split(jax.random.key(seed), 6)
    part_splits = jax.random.split(jax.random.fold_in(key_list[5], part), 6)
    return {
        "psi": centred(part_splits[0], (NB, V, P_SIZE, P_SIZE), 1.0, 6.0, ((0, 4),)),
        "left_env": centred(part_splits[1], (K, NB, P_SIZE, P_SIZE), P_SIZE ** -0.5, 0.375, ((0, 4), (1, 4))),
        "right_env": centred(part_splits[2], (K, NB, P_SIZE, P_SIZE), (P_SIZE * K) ** -0.5, 0.125, ((0, 4), (1, 4))),
        "sector_dims": draw_sector_dims(jax.random.fold_in(jax.random.fold_in(key_list[5], part), 71), part),
        "right_place": draw_right_place(jax.random.fold_in(jax.random.fold_in(key_list[5], part), 71), part),
    }


def reference(psi, left_env, right_env, sector_dims, right_place):
    cols = jnp.arange(P_SIZE, dtype=jnp.int32)

    def one_block(index):
        rows_ok = cols < sector_dims[0, index]
        cols_ok = cols < sector_dims[1, index]
        keep = rows_ok[None, :, None] & cols_ok[None, None, :]
        block = jnp.where(keep, psi[index], jnp.zeros_like(psi[index])).astype(jnp.float32)
        left_part = lax.dynamic_index_in_dim(left_env, index, 1, keepdims=False).astype(jnp.float32)
        right_part = lax.dynamic_index_in_dim(right_env, right_place[index], 1, keepdims=False).astype(jnp.float32)
        trans = jnp.einsum("kpq,vqr->kvpr", left_part, block).astype(jnp.bfloat16)
        trans = lax.optimization_barrier(trans).astype(jnp.float32)
        total = jnp.einsum("kvpq,kqr->vpr", trans, right_part)
        total = jnp.where(keep, total, jnp.zeros_like(total))
        return total.astype(jnp.bfloat16)

    blocks = lax.map(one_block, jnp.arange(NB, dtype=jnp.int32))
    return jnp.zeros_like(psi).at[right_place].set(blocks)
```

```python
import functools

import jax
import jax.numpy as jnp
from jax import lax
from jax.experimental import pallas as pl
from jax.experimental.pallas import tpu as pltpu
from jax.sharding import PartitionSpec as P

ANY = pl.BlockSpec(memory_space=pl.ANY)
SMEM = pl.BlockSpec(memory_space=pltpu.SMEM)
VMEM = pl.BlockSpec(memory_space=pltpu.VMEM)


def peer(i, d, n):
    return i ^ d if n & (n - 1) == 0 else (i + d) % n


def back(i, d, n):
    return i ^ d if n & (n - 1) == 0 else (i + n - d) % n


def find(place, nb, left, right):
    block, slot, found = jnp.int32(0), jnp.int32(0), jnp.bool_(False)
    for i in range(nb):
        at = place[left * nb + i]
        hit = lax.div(at, jnp.int32(nb)) == right
        block = jnp.where(hit, jnp.int32(i), block)
        slot = jnp.where(hit, lax.rem(at, jnp.int32(nb)), slot)
        found = found | hit
    return block, slot, found


def pick_kernel(nsec, nb, place, right_env, *rest):
    outs, sems = rest[:-1], rest[-1]
    me = lax.axis_index("sec")
    copies = []
    for n, d in enumerate(range(1, nsec)):
        _, slot, _ = find(place, nb, peer(me, d, nsec), me)
        copies.append(pltpu.make_async_copy(right_env.at[:, slot], outs[n], sems.at[n]))
        copies[-1].start()
    for copy in copies:
        copy.wait()


def work_kernel(rounds, nsec, nop, nb, place, dims, psi, left_env, *rest):
    count = len(rounds)
    rights, rest = rest[:count], rest[count:]
    keep, sends, rest = rest[0], rest[1:nop], rest[nop:]
    psi_v, left_v, right_v, total, sems = rest
    me = lax.axis_index("sec")
    mine = lax.axis_index("op")
    terms, vecs, width = left_v.shape[1], psi_v.shape[1], psi_v.shape[-1]
    rows = width // nop
    places, copies = [], []
    for e, d in enumerate(rounds):
        block, slot, found = find(place, nb, me, back(me, d, nsec))
        places.append((block, found))
        right = rights[e].at[:, slot] if d == 0 else rights[e]
        group = [
            pltpu.make_async_copy(psi.at[block], psi_v.at[e], sems.at[e, 0]),
            pltpu.make_async_copy(left_env.at[:, block], left_v.at[e], sems.at[e, 1]),
            pltpu.make_async_copy(right, right_v.at[e], sems.at[e, 2]),
        ]
        for copy in group:
            copy.start()
        copies.append(group)
    row = lax.broadcasted_iota(jnp.int32, (width, width), 0)
    col = lax.broadcasted_iota(jnp.int32, (width, width), 1)
    for e in range(count):
        block, found = places[e]
        live_rows = jnp.where(found, dims[0, me * nb + block], 0)
        live_cols = jnp.where(found, dims[1, me * nb + block], 0)
        keep_block = (row < live_rows) & (col < live_cols)
        copies[e][0].wait()
        copies[e][1].wait()
        masked = [jnp.where(keep_block, psi_v[e, v], jnp.zeros_like(psi_v[e, v])) for v in range(vecs)]
        trans = [
            [
                jnp.dot(left_v[e, k], masked[v], preferred_element_type=jnp.float32).astype(jnp.bfloat16)
                for k in range(terms)
            ]
            for v in range(vecs)
        ]
        copies[e][2].wait()
        for v in range(vecs):
            value = jnp.dot(trans[v][0], right_v[e, 0], preferred_element_type=jnp.float32)
            for k in range(1, terms):
                value = value + jnp.dot(trans[v][k], right_v[e, k], preferred_element_type=jnp.float32)
            total[v] = jnp.where(keep_block, value, 0.0)
        for d in range(nop):
            start = pl.multiple_of(peer(mine, d, nop) * rows, rows)
            part = total[:, pl.ds(start, rows), :]
            if d == 0:
                keep[e] = part
            else:
                sends[d - 1][e] = part.astype(jnp.bfloat16)


def place_kernel(nsec, nb, place, *rest):
    parts, out = rest[:-1], rest[-1]
    me = lax.axis_index("sec")
    for d in range(nsec):
        _, slot, found = find(place, nb, peer(me, d, nsec), me)

        @pl.when(found)
        def _():
            out[slot] = parts[d][...]


def local(psi, left_env, right_env, sector_dims, right_place):
    nsec, nop = lax.axis_size("sec"), lax.axis_size("op")
    nb, vecs, width, _ = psi.shape
    terms = left_env.shape[0]
    rows = width // nop
    block = width * width

    def ship(x, axis, way, d):
        n = lax.axis_size(axis)
        return lax.ppermute(x, axis, [(i, way(i, d, n)) for i in range(n)])

    picked = pl.pallas_call(
        functools.partial(pick_kernel, nsec, nb),
        in_specs=[SMEM, ANY],
        out_specs=[ANY] * (nsec - 1),
        out_shape=[jax.ShapeDtypeStruct((terms, width, width), right_env.dtype)] * (nsec - 1),
        scratch_shapes=[pltpu.SemaphoreType.DMA((nsec - 1,))],
        cost_estimate=pl.CostEstimate(flops=0, bytes_accessed=4 * nsec * terms * block, transcendentals=0),
        name="pick",
    )(right_place, right_env)
    rights = [right_env] + [ship(picked[d - 1], "sec", peer, d) for d in range(1, nsec)]

    def work(rounds):
        count = len(rounds)
        outs = pl.pallas_call(
            functools.partial(work_kernel, rounds, nsec, nop, nb),
            in_specs=[SMEM, SMEM, ANY, ANY] + [ANY] * count,
            out_specs=[VMEM] * nop,
            out_shape=[jax.ShapeDtypeStruct((count, vecs, rows, width), jnp.float32)]
            + [jax.ShapeDtypeStruct((count, vecs, rows, width), jnp.bfloat16)] * (nop - 1),
            scratch_shapes=[
                pltpu.VMEM((count, vecs, width, width), jnp.bfloat16),
                pltpu.VMEM((count, terms, width, width), jnp.bfloat16),
                pltpu.VMEM((count, terms, width, width), jnp.bfloat16),
                pltpu.VMEM((vecs, width, width), jnp.float32),
                pltpu.SemaphoreType.DMA((count, 3)),
            ],
            compiler_params=pltpu.CompilerParams(vmem_limit_bytes=48 * 2**20),
            cost_estimate=pl.CostEstimate(
                flops=count * terms * vecs * 4 * width**3,
                bytes_accessed=count * block * 2 * (2 * terms + 2 * vecs),
                transcendentals=0,
            ),
            name="work",
        )(right_place, sector_dims, psi, left_env, *[rights[d] for d in rounds])
        value = outs[0]
        for d in range(1, nop):
            value = value + ship(outs[d], "op", peer, d).astype(jnp.float32)
        return value.astype(jnp.bfloat16)

    groups = [[d] for d in range(nsec)] if nsec <= 4 else [list(range(nsec // 2)), list(range(nsec // 2, nsec))]
    parts = []
    for rounds in groups:
        value = work(rounds)
        for e, d in enumerate(rounds):
            parts.append(value[e] if d == 0 else ship(value[e], "sec", back, d))

    return pl.pallas_call(
        functools.partial(place_kernel, nsec, nb),
        in_specs=[SMEM] + [VMEM] * nsec,
        out_specs=VMEM,
        out_shape=jax.ShapeDtypeStruct((nb, vecs, rows, width), jnp.bfloat16),
        name="place",
    )(right_place, *parts)


def solution(mesh):
    return jax.shard_map(
        local,
        mesh=mesh,
        in_specs=(
            P(("grp", "sec"), None, None, None),
            P("op", ("grp", "sec"), None, None),
            P("op", ("grp", "sec"), None, None),
            P(None, "grp"),
            P("grp"),
        ),
        out_specs=P(("grp", "sec"), None, "op", None),
        check_vma=False,
    )
```

```python
import functools

import jax
import jax.numpy as jnp
from jax import lax
from jax.experimental import pallas as pl
from jax.experimental.pallas import tpu as pltpu
from jax.sharding import PartitionSpec as P

ANY = pl.BlockSpec(memory_space=pl.ANY)
HBM = pl.BlockSpec(memory_space=pltpu.HBM)
SMEM = pl.BlockSpec(memory_space=pltpu.SMEM)
VMEM = pl.BlockSpec(memory_space=pltpu.VMEM)
F32 = jnp.float32
BF16 = jnp.bfloat16


def peer(i, d, n):
    return i ^ d if n & (n - 1) == 0 else (i + d) % n


def back(i, d, n):
    return i ^ d if n & (n - 1) == 0 else (i + n - d) % n


def find(place, nb, left, right):
    block, slot, found = jnp.int32(0), jnp.int32(0), jnp.bool_(False)
    for i in range(nb):
        at = place[left * nb + i]
        hit = lax.div(at, jnp.int32(nb)) == right
        block = jnp.where(hit, jnp.int32(i), block)
        slot = jnp.where(hit, lax.rem(at, jnp.int32(nb)), slot)
        found = found | hit
    return block, slot, found


def chunk(ref, lead, index, rows):
    return ref.at[(*lead, pl.ds(pl.multiple_of(index * rows, rows), rows))]


def run(copies):
    for copy in copies:
        copy.start()
    return copies


def pick_kernel(nsec, nop, nb, place, psi, left_env, *rest):
    outs, sems = rest[:-1], rest[-1]
    me, mine = lax.axis_index("sec"), lax.axis_index("op")
    rows = psi.shape[-2] // nop
    every = slice(None)
    copies = []
    for n in range(nsec - 1):
        piece, others, own = outs[n], outs[nsec - 1 + n], outs[2 * (nsec - 1) + n]
        block, _, _ = find(place, nb, me, peer(me, n + 1, nsec))
        sources = [(chunk(psi, (block, every), mine, rows), piece)]
        for o in range(1, nop):
            at = pl.ds((o - 1) * rows, rows)
            sources.append((chunk(left_env, (every, block), peer(mine, o, nop), rows), others.at[:, at]))
        sources.append((chunk(left_env, (every, block), mine, rows), own))
        for m, (src, dst) in enumerate(sources):
            copies.append(pltpu.make_async_copy(src, dst, sems.at[n, m]))
    for copy in run(copies):
        copy.wait()


def mask_kernel(nsec, nop, nb, place, dims, psi, *rest):
    pieces, out, sems = rest[:nop], rest[nop], rest[nop + 1]
    me, mine = lax.axis_index("sec"), lax.axis_index("op")
    rows, width = out.shape[-2] // nop, out.shape[-1]
    every = slice(None)
    block, _, _ = find(place, nb, me, me)
    copies = [[pltpu.make_async_copy(psi.at[block], out.at[0], sems.at[0, 0])]]
    for d in range(1, nsec):
        copies.append(
            [
                pltpu.make_async_copy(
                    pieces[o].at[d - 1], chunk(out, (d, every), back(mine, o, nop), rows), sems.at[d, o]
                )
                for o in range(nop)
            ]
        )
    for group in copies:
        run(group)
    row = lax.broadcasted_iota(jnp.int32, (width, width), 0)
    col = lax.broadcasted_iota(jnp.int32, (width, width), 1)
    for d in range(nsec):
        source = back(me, d, nsec)
        block, _, found = find(place, nb, source, me)
        live_rows = jnp.where(found, dims[0, source * nb + block], 0)
        live_cols = jnp.where(found, dims[1, source * nb + block], 0)
        alive = (row < live_rows) & (col < live_cols)
        for copy in copies[d]:
            copy.wait()
        for v in range(out.shape[1]):
            out[d, v] = jnp.where(alive, out[d, v], jnp.zeros_like(out[d, v]))


def both(left, masked, right, terms, vecs):
    values = []
    for v in range(vecs):
        value = None
        for k in range(terms):
            trans = jnp.dot(left(k), masked(v), preferred_element_type=F32).astype(BF16)
            term = jnp.dot(trans, right(k), preferred_element_type=F32)
            value = term if value is None else value + term
        values.append(value)
    return values


def others_kernel(rounds, nsec, nop, nb, place, dims, masked, right_env, left_env, *rest):
    count = len(rounds)
    given = count - (0 in rounds)
    lefts, sends, rest = rest[:given], rest[given : given + nop - 1], rest[given + nop - 1 :]
    masked_v, left_v, right_v, sems = rest
    me, mine = lax.axis_index("sec"), lax.axis_index("op")
    terms, vecs, width = left_v.shape[1], masked_v.shape[1], masked_v.shape[-1]
    rows = width // nop
    every = slice(None)
    copies = []
    for e, d in enumerate(rounds):
        block, slot, _ = find(place, nb, back(me, d, nsec), me)
        group = [
            pltpu.make_async_copy(masked.at[d], masked_v.at[e], sems.at[e, 0]),
            pltpu.make_async_copy(right_env.at[:, slot], right_v.at[e], sems.at[e, 1]),
        ]
        if d == 0:
            for o in range(1, nop):
                src = chunk(left_env, (every, block), peer(mine, o, nop), rows)
                dst = left_v.at[e, :, pl.ds((o - 1) * rows, rows)]
                group.append(pltpu.make_async_copy(src, dst, sems.at[e, 1 + o]))
        else:
            group.append(pltpu.make_async_copy(lefts[e - (0 in rounds)], left_v.at[e], sems.at[e, 2]))
        copies.append(run(group))
    row = lax.broadcasted_iota(jnp.int32, (rows, width), 0)
    col = lax.broadcasted_iota(jnp.int32, (rows, width), 1)
    for e, d in enumerate(rounds):
        source = back(me, d, nsec)
        block, _, found = find(place, nb, source, me)
        live_rows = jnp.where(found, dims[0, source * nb + block], 0)
        live_cols = jnp.where(found, dims[1, source * nb + block], 0)
        for copy in copies[e]:
            copy.wait()
        values = both(lambda k: left_v[e, k], lambda v: masked_v[e, v], lambda k: right_v[e, k], terms, vecs)
        for o in range(1, nop):
            alive = (row + peer(mine, o, nop) * rows < live_rows) & (col < live_cols)
            for v in range(vecs):
                part = values[v][(o - 1) * rows : o * rows]
                sends[o - 1][e, v] = jnp.where(alive, part, 0.0).astype(BF16)


def own_kernel(groups, nsec, nop, nb, place, dims, masked, right_env, left_env, *rest):
    lefts, rest = rest[: nsec - 1], rest[nsec - 1 :]
    heard, rest = rest[: len(groups) * (nop - 1)], rest[len(groups) * (nop - 1) :]
    out, masked_v, left_v, right_v, heard_v, sems = rest
    me, mine = lax.axis_index("sec"), lax.axis_index("op")
    terms, vecs, width = left_v.shape[1], masked_v.shape[1], masked_v.shape[-1]
    rows = width // nop
    every = slice(None)
    copies = []
    for d in range(nsec):
        block, slot, _ = find(place, nb, back(me, d, nsec), me)
        left = chunk(left_env, (every, block), mine, rows) if d == 0 else lefts[d - 1]
        copies.append(
            [
                pltpu.make_async_copy(masked.at[d], masked_v.at[d], sems.at[d, 0]),
                pltpu.make_async_copy(right_env.at[:, slot], right_v.at[d], sems.at[d, 1]),
                pltpu.make_async_copy(left, left_v.at[d], sems.at[d, 2]),
            ]
        )
        for g, rounds in enumerate(groups):
            if d in rounds:
                for o in range(nop - 1):
                    src = heard[g * (nop - 1) + o].at[rounds.index(d)]
                    copies[-1].append(pltpu.make_async_copy(src, heard_v.at[d, o], sems.at[d, 3 + o]))
    for group in copies:
        run(group)
    row = lax.broadcasted_iota(jnp.int32, (rows, width), 0) + mine * rows
    col = lax.broadcasted_iota(jnp.int32, (rows, width), 1)
    for d in range(nsec):
        source = back(me, d, nsec)
        block, slot, found = find(place, nb, source, me)
        live_rows = jnp.where(found, dims[0, source * nb + block], 0)
        live_cols = jnp.where(found, dims[1, source * nb + block], 0)
        alive = (row < live_rows) & (col < live_cols)
        for copy in copies[d]:
            copy.wait()
        values = both(lambda k: left_v[d, k], lambda v: masked_v[d, v], lambda k: right_v[d, k], terms, vecs)
        sums = []
        for v in range(vecs):
            value = jnp.where(alive, values[v], 0.0)
            for o in range(nop - 1):
                value = value + heard_v[d, o, v].astype(F32)
            sums.append(value.astype(BF16))

        @pl.when(found)
        def _():
            for v in range(vecs):
                out[slot, v] = sums[v]


def local(psi, left_env, right_env, sector_dims, right_place):
    nsec, nop = lax.axis_size("sec"), lax.axis_size("op")
    nb, vecs, width, _ = psi.shape
    terms = left_env.shape[0]
    rows = width // nop
    away = nsec - 1
    params = pltpu.CompilerParams(vmem_limit_bytes=40 * 2**20)
    shape = lambda *dims: jax.ShapeDtypeStruct(dims, BF16)
    dma = lambda *dims: pltpu.SemaphoreType.DMA(dims)

    def ship(x, axis, d):
        n = lax.axis_size(axis)
        return lax.ppermute(x, axis, [(i, peer(i, d, n)) for i in range(n)])

    def cost(flops, values):
        return pl.CostEstimate(flops=flops, bytes_accessed=2 * values, transcendentals=0)

    picked = pl.pallas_call(
        functools.partial(pick_kernel, nsec, nop, nb),
        in_specs=[SMEM, HBM, HBM],
        out_specs=[VMEM] * (3 * away),
        out_shape=[shape(vecs, rows, width)] * away
        + [shape(terms, width - rows, width)] * away
        + [shape(terms, rows, width)] * away,
        scratch_shapes=[dma(away, nop + 1)],
        compiler_params=params,
        cost_estimate=cost(0, 2 * away * terms * width * width),
        name="pick",
    )(right_place, psi, left_env)

    pieces = [ship(picked[d - 1], "sec", d) for d in range(1, nsec)]
    lefts_others = [ship(picked[away + d - 1], "sec", d) for d in range(1, nsec)]
    lefts_own = [ship(picked[2 * away + d - 1], "sec", d) for d in range(1, nsec)]

    gathered = {0: jnp.stack(pieces)}
    if nop & (nop - 1) == 0:
        bit = nop // 2
        while bit:
            for o in sorted(gathered):
                gathered[o ^ bit] = ship(gathered[o], "op", bit)
            bit //= 2
    else:
        for o in range(1, nop):
            gathered[o] = ship(gathered[0], "op", o)

    masked = pl.pallas_call(
        functools.partial(mask_kernel, nsec, nop, nb),
        in_specs=[SMEM, SMEM, HBM] + [ANY] * nop,
        out_specs=VMEM,
        out_shape=shape(nsec, vecs, width, width),
        scratch_shapes=[dma(nsec, nop)],
        compiler_params=params,
        cost_estimate=cost(0, 2 * nsec * vecs * width * width),
        name="mask",
    )(right_place, sector_dims, psi, *[gathered[o] for o in range(nop)])

    groups = [[0, 1], [2], [3]] if nsec == 4 else [list(range(nsec // 2)), list(range(nsec // 2, nsec))]
    heard = []
    for rounds in groups:
        count = len(rounds)
        given = [lefts_others[d - 1] for d in rounds if d]
        sends = pl.pallas_call(
            functools.partial(others_kernel, rounds, nsec, nop, nb),
            in_specs=[SMEM, SMEM, ANY, HBM, HBM] + [ANY] * len(given),
            out_specs=[VMEM] * (nop - 1),
            out_shape=[shape(count, vecs, rows, width)] * (nop - 1),
            scratch_shapes=[
                pltpu.VMEM((count, vecs, width, width), BF16),
                pltpu.VMEM((count, terms, width - rows, width), BF16),
                pltpu.VMEM((count, terms, width, width), BF16),
                dma(count, nop + 1),
            ],
            compiler_params=params,
            cost_estimate=cost(count * terms * vecs * 3 * width**3, count * width * width * (2 * terms + 2 * vecs)),
            name="others",
        )(right_place, sector_dims, masked, right_env, left_env, *given)
        heard += [ship(sends[o - 1], "op", o) for o in range(1, nop)]

    return pl.pallas_call(
        functools.partial(own_kernel, groups, nsec, nop, nb),
        in_specs=[SMEM, SMEM, ANY, HBM, HBM] + [ANY] * (away + len(heard)),
        out_specs=VMEM,
        out_shape=shape(nb, vecs, rows, width),
        scratch_shapes=[
            pltpu.VMEM((nsec, vecs, width, width), BF16),
            pltpu.VMEM((nsec, terms, rows, width), BF16),
            pltpu.VMEM((nsec, terms, width, width), BF16),
            pltpu.VMEM((nsec, nop - 1, vecs, rows, width), BF16),
            dma(nsec, nop + 2),
        ],
        compiler_params=params,
        cost_estimate=cost(nsec * terms * vecs * width**3, nsec * width * width * (2 * terms + 2 * vecs)),
        name="own",
    )(right_place, sector_dims, masked, right_env, left_env, *lefts_own, *heard)


def solution(mesh):
    return jax.shard_map(
        local,
        mesh=mesh,
        in_specs=(
            P(("grp", "sec"), None, None, None),
            P("op", ("grp", "sec"), None, None),
            P("op", ("grp", "sec"), None, None),
            P(None, "grp"),
            P("grp"),
        ),
        out_specs=P(("grp", "sec"), None, "op", None),
        check_vma=False,
    )
```

```python
import functools

import jax
import jax.numpy as jnp
from jax import lax
from jax.experimental import pallas as pl
from jax.experimental.pallas import tpu as pltpu
from jax.sharding import PartitionSpec as P

ANY = pl.BlockSpec(memory_space=pl.ANY)
HBM = pl.BlockSpec(memory_space=pltpu.HBM)
SMEM = pl.BlockSpec(memory_space=pltpu.SMEM)
VMEM = pl.BlockSpec(memory_space=pltpu.VMEM)
F32 = jnp.float32
BF16 = jnp.bfloat16
EVERY = slice(None)
LONG = 10**11


def peer(i, d, n):
    return i ^ d if n & (n - 1) == 0 else (i + d) % n


def back(i, d, n):
    return i ^ d if n & (n - 1) == 0 else (i + n - d) % n


def find(place, nb, left, right):
    block, slot, found = jnp.int32(0), jnp.int32(0), jnp.bool_(False)
    for i in range(nb):
        at = place[left * nb + i]
        hit = lax.div(at, jnp.int32(nb)) == right
        block = jnp.where(hit, jnp.int32(i), block)
        slot = jnp.where(hit, lax.rem(at, jnp.int32(nb)), slot)
        found = found | hit
    return block, slot, found


def chunk(ref, lead, index, rows):
    return ref.at[(*lead, pl.ds(pl.multiple_of(index * rows, rows), rows))]


class Copies:
    def __init__(self, sems):
        self.sems, self.used, self.groups = sems, 0, {}

    def add(self, group, src, dst):
        copy = pltpu.make_async_copy(src, dst, self.sems.at[self.used])
        self.used += 1
        copy.start()
        self.groups.setdefault(group, []).append(copy)

    def wait(self, group):
        for copy in self.groups.pop(group):
            copy.wait()


def pick_kernel(nsec, nop, nb, place, psi, left_env, *rest):
    outs, copies = rest[:-1], Copies(rest[-1])
    me, mine = lax.axis_index("sec"), lax.axis_index("op")
    terms, vecs = left_env.shape[0], psi.shape[1]
    rows = psi.shape[-2] // nop
    found = [find(place, nb, me, peer(me, d, nsec))[0] for d in range(1, nsec)]
    for n in range(1, nsec - 1):
        copies.add(0, chunk(psi, (found[n], EVERY), mine, rows), outs[n])
    copies.add(0, psi.at[found[0]], outs[0].at[pl.ds(0, vecs)])
    copies.add(0, left_env.at[:, found[0]], outs[0].at[pl.ds(vecs, terms)])
    for n in range(1, nsec - 1):
        copies.add(0, left_env.at[:, found[n]], outs[nsec - 2 + n])
    copies.wait(0)


def stack_kernel(*refs):
    pieces, out, copies = refs[:-2], refs[-2], Copies(refs[-1])
    for n, piece in enumerate(pieces):
        copies.add(0, piece, out.at[n])
    copies.wait(0)


def work_kernel(rounds, waits, nsec, nop, nb, place, dims, psi, left_env, right_env, near, *rest):
    count = len(rounds)
    far = [d for d in rounds if d > 1]
    pieces, rest = (rest[:nop], rest[nop:]) if far else ((), rest)
    rest = rest[waits:]
    lefts, rest = rest[: len(far)], rest[len(far) :]
    keep, sends, rest = rest[0], rest[1:nop], rest[nop:]
    psi_v, left_v, right_v, total, sems = rest
    copies = Copies(sems)
    me, mine = lax.axis_index("sec"), lax.axis_index("op")
    terms, vecs, width = left_v.shape[1], psi_v.shape[1], psi_v.shape[-1]
    rows = width // nop
    found = [find(place, nb, back(me, d, nsec), me) for d in rounds]
    for e, d in enumerate(rounds):
        block, slot, _ = found[e]
        if d == 0:
            copies.add((e, 0), psi.at[block], psi_v.at[e])
            copies.add((e, 0), left_env.at[:, block], left_v.at[e])
        elif d == 1:
            copies.add((e, 0), near.at[pl.ds(0, vecs)], psi_v.at[e])
            copies.add((e, 0), near.at[pl.ds(vecs, terms)], left_v.at[e])
        else:
            for o in range(nop):
                copies.add((e, 0), pieces[o].at[d - 2], chunk(psi_v, (e, EVERY), back(mine, o, nop), rows))
            copies.add((e, 0), lefts[far.index(d)], left_v.at[e])
        copies.add((e, 1), right_env.at[:, slot], right_v.at[e])
    row = lax.broadcasted_iota(jnp.int32, (width, width), 0)
    col = lax.broadcasted_iota(jnp.int32, (width, width), 1)
    for e, d in enumerate(rounds):
        block, _, there = found[e]
        source = back(me, d, nsec)
        live_rows = jnp.where(there, dims[0, source * nb + block], 0)
        live_cols = jnp.where(there, dims[1, source * nb + block], 0)
        alive = (row < live_rows) & (col < live_cols)
        copies.wait((e, 0))
        left = left_v[e].reshape(terms * width, width)
        trans = []
        for v in range(vecs):
            masked = jnp.where(alive, psi_v[e, v], jnp.zeros_like(psi_v[e, v]))
            trans.append(jnp.dot(left, masked, preferred_element_type=F32).astype(BF16))
        copies.wait((e, 1))
        for v in range(vecs):
            value = None
            for k in range(terms):
                term = jnp.dot(trans[v][k * width : (k + 1) * width], right_v[e, k], preferred_element_type=F32)
                value = term if value is None else value + term
            total[v] = jnp.where(alive, value, 0.0)
        for o in range(nop):
            start = pl.multiple_of(peer(mine, o, nop) * rows, rows)
            part = total[:, pl.ds(start, rows), :]
            if o == 0:
                keep[e] = part
            else:
                sends[o - 1][e] = part.astype(BF16)


def final_kernel(groups, nsec, nop, nb, place, *rest):
    ready, keep, heard, rest = rest[: len(groups) - 1], rest[len(groups) - 1], rest[len(groups) : -5], rest[-5:]
    out, ready_v, keep_v, heard_v, sems = rest
    copies = Copies(sems)
    me = lax.axis_index("sec")
    count = keep.shape[0]
    copies.add("last", keep, keep_v)
    for n, part in enumerate(heard):
        copies.add("last", part, heard_v.at[n])
    at = 0
    for n, part in enumerate(ready):
        copies.add("ready", part, ready_v.at[pl.ds(at, part.shape[0])])
        at += part.shape[0]
    copies.wait("ready")

    def store(d, value):
        _, slot, there = find(place, nb, back(me, d, nsec), me)

        @pl.when(there)
        def _():
            out[slot] = value

    for n, d in enumerate(d for rounds in groups[:-1] for d in rounds):
        store(d, ready_v[n])
    copies.wait("last")
    for e, d in enumerate(groups[-1]):
        value = keep_v[e]
        for o in range(nop - 1):
            value = value + heard_v[o, e].astype(F32)
        store(d, value.astype(BF16))


def local(psi, left_env, right_env, sector_dims, right_place):
    nsec, nop = lax.axis_size("sec"), lax.axis_size("op")
    nb, vecs, width, _ = psi.shape
    terms = left_env.shape[0]
    rows = width // nop
    far = nsec - 2
    params = pltpu.CompilerParams(vmem_limit_bytes=40 * 2**20)
    shape = lambda *dims: jax.ShapeDtypeStruct(dims, BF16)
    dma = lambda *dims: pltpu.SemaphoreType.DMA(dims)

    def ship(x, axis, d):
        n = lax.axis_size(axis)
        return lax.ppermute(x, axis, [(i, peer(i, d, n)) for i in range(n)])

    def cost(flops, values):
        return pl.CostEstimate(flops=flops, bytes_accessed=2 * values, transcendentals=0)

    picked = pl.pallas_call(
        functools.partial(pick_kernel, nsec, nop, nb),
        in_specs=[SMEM, HBM, HBM],
        out_specs=[VMEM] * (1 + 2 * far),
        out_shape=[shape(vecs + terms, width, width)]
        + [shape(vecs, rows, width)] * far
        + [shape(terms, width, width)] * far,
        scratch_shapes=[dma(2 + 2 * far)],
        compiler_params=pltpu.CompilerParams(vmem_limit_bytes=PICK * 2**20),
        cost_estimate=cost(0, 2 * nsec * terms * width * width),
        name="pick",
    )(right_place, psi, left_env)

    pieces = [ship(picked[d - 1], "sec", d) for d in range(2, nsec)]
    near = ship(picked[0], "sec", 1)
    lefts = {d: ship(picked[far + d - 1], "sec", d) for d in range(2, nsec)}

    stacked = pl.pallas_call(
        stack_kernel,
        in_specs=[ANY] * far,
        out_specs=VMEM,
        out_shape=shape(far, vecs, rows, width),
        scratch_shapes=[dma(far)],
        compiler_params=params,
        cost_estimate=cost(STACK, 0),
        name="stack",
    )(*pieces)
    gathered = {0: stacked}
    if nop & (nop - 1) == 0:
        bit = nop // 2
        while bit:
            for o in sorted(gathered):
                gathered[o ^ bit] = ship(gathered[o], "op", bit)
            bit //= 2
    else:
        for o in range(1, nop):
            gathered[o] = ship(stacked, "op", o)

    half = 2 + far // 2
    groups = [[0, 1], list(range(2, half)), list(range(half, nsec))]
    after, ready = [], []
    for rounds in groups:
        count = len(rounds)
        given = [lefts[d] for d in rounds if d > 1]
        if given:
            given = [gathered[o] for o in range(nop)] + list(after) + given
        outs = pl.pallas_call(
            functools.partial(work_kernel, rounds, len(after), nsec, nop, nb),
            in_specs=[SMEM, SMEM, HBM, HBM, HBM] + [ANY] * (1 + len(given)),
            out_specs=[VMEM] * nop,
            out_shape=[jax.ShapeDtypeStruct((count, vecs, rows, width), F32)]
            + [shape(count, vecs, rows, width)] * (nop - 1),
            scratch_shapes=[
                pltpu.VMEM((count, vecs, width, width), BF16),
                pltpu.VMEM((count, terms, width, width), BF16),
                pltpu.VMEM((count, terms, width, width), BF16),
                pltpu.VMEM((vecs, width, width), F32),
                dma(count * (nop + 2)),
            ],
            compiler_params=params,
            cost_estimate=cost(WORK, 0),
            name="work",
        )(right_place, sector_dims, psi, left_env, right_env, near, *given)
        after = [outs[1]]
        heard = [ship(outs[o], "op", o) for o in range(1, nop)]
        if rounds is not groups[-1]:
            value = outs[0]
            for part in heard:
                value = value + part.astype(F32)
            ready.append(value.astype(BF16))

    count = len(groups[-1])
    return pl.pallas_call(
        functools.partial(final_kernel, groups, nsec, nop, nb),
        in_specs=[SMEM] + [ANY] * (len(ready) + nop),
        out_specs=VMEM,
        out_shape=shape(nb, vecs, rows, width),
        scratch_shapes=[
            pltpu.VMEM((nsec - count, vecs, rows, width), BF16),
            pltpu.VMEM((count, vecs, rows, width), F32),
            pltpu.VMEM((nop - 1, count, vecs, rows, width), BF16),
            dma(len(ready) + nop),
        ],
        compiler_params=params,
        cost_estimate=cost(0, 0),
        name="final",
    )(right_place, *ready, outs[0], *heard)


PICK, STACK, WORK = 61, 0, 0


def solution(mesh):
    return jax.shard_map(
        local,
        mesh=mesh,
        in_specs=(
            P(("grp", "sec"), None, None, None),
            P("op", ("grp", "sec"), None, None),
            P("op", ("grp", "sec"), None, None),
            P(None, "grp"),
            P("grp"),
        ),
        out_specs=P(("grp", "sec"), None, "op", None),
        check_vma=False,
    )
```

```python
import functools

import jax
import jax.numpy as jnp
from jax import lax
from jax.experimental import pallas as pl
from jax.experimental.pallas import tpu as pltpu
from jax.sharding import PartitionSpec as P

ANY = pl.BlockSpec(memory_space=pl.ANY)
HBM = pl.BlockSpec(memory_space=pltpu.HBM)
SMEM = pl.BlockSpec(memory_space=pltpu.SMEM)
VMEM = pl.BlockSpec(memory_space=pltpu.VMEM)
F32 = jnp.float32
BF16 = jnp.bfloat16
EVERY = slice(None)
LONG = 10**11


def find(place, nb, left, right):
    block, slot, found = jnp.int32(0), jnp.int32(0), jnp.bool_(False)
    for i in range(nb):
        at = place[left * nb + i]
        hit = lax.div(at, jnp.int32(nb)) == right
        block = jnp.where(hit, jnp.int32(i), block)
        slot = jnp.where(hit, lax.rem(at, jnp.int32(nb)), slot)
        found = found | hit
    return block, slot, found


def chunk(ref, lead, index, rows):
    return ref.at[(*lead, pl.ds(pl.multiple_of(index * rows, rows), rows))]


class Copies:
    def __init__(self, sems):
        self.sems, self.used, self.groups = sems, 0, {}

    def add(self, group, src, dst):
        copy = pltpu.make_async_copy(src, dst, self.sems.at[self.used])
        self.used += 1
        copy.start()
        self.groups.setdefault(group, []).append(copy)

    def wait(self, group):
        for copy in self.groups.pop(group):
            copy.wait()


def pick_kernel(nsec, nop, nb, place, psi, left_env, *rest):
    outs, copies = rest[:-1], Copies(rest[-1])
    me, mine = lax.axis_index("sec"), lax.axis_index("op")
    found = [find(place, nb, me, me ^ d)[0] for d in range(1, nsec)]
    for n, block in enumerate(found):
        copies.add(0, left_env.at[:, block], outs[nsec - 1 + n])
    for n, block in enumerate(found):
        copies.add(0, chunk(psi, (block, EVERY), mine, psi.shape[-2] // nop), outs[n])
    copies.wait(0)


def stack_kernel(*refs):
    pieces, out, copies = refs[:-2], refs[-2], Copies(refs[-1])
    for n, piece in enumerate(pieces):
        copies.add(0, piece, out.at[n])
    copies.wait(0)


def work_kernel(rounds, waits, nsec, nop, nb, place, dims, psi, left_env, right_env, *rest):
    count = len(rounds)
    far = [d for d in rounds if d]
    rest = rest[waits:]
    pieces, rest = (rest[:nop], rest[nop:]) if far else ((), rest)
    lefts, rest = rest[: len(far)], rest[len(far) :]
    keep, send, psi_v, left_v, right_v, total, sems = rest
    copies = Copies(sems)
    me, mine = lax.axis_index("sec"), lax.axis_index("op")
    terms, vecs, width = left_v.shape[1], psi_v.shape[1], psi_v.shape[-1]
    rows = width // nop
    found = [find(place, nb, me ^ d, me) for d in rounds]
    for e, d in enumerate(rounds):
        block, slot, _ = found[e]
        if d == 0:
            copies.add((e, 0), psi.at[block], psi_v.at[e])
            copies.add((e, 0), left_env.at[:, block], left_v.at[e])
        else:
            for o in range(nop):
                copies.add((e, 0), pieces[o].at[d - 1], chunk(psi_v, (e, EVERY), mine ^ o, rows))
            copies.add((e, 0), lefts[far.index(d)], left_v.at[e])
        copies.add((e, 1), right_env.at[:, slot], right_v.at[e])
    row = lax.broadcasted_iota(jnp.int32, (width, width), 0)
    col = lax.broadcasted_iota(jnp.int32, (width, width), 1)
    for e, d in enumerate(rounds):
        block, _, there = found[e]
        source = me ^ d
        live_rows = jnp.where(there, dims[0, source * nb + block], 0)
        live_cols = jnp.where(there, dims[1, source * nb + block], 0)
        alive = (row < live_rows) & (col < live_cols)
        copies.wait((e, 0))
        left = left_v[e].reshape(terms * width, width)
        trans = []
        for v in range(vecs):
            masked = jnp.where(alive, psi_v[e, v], jnp.zeros_like(psi_v[e, v]))
            trans.append(jnp.dot(left, masked, preferred_element_type=F32).astype(BF16))
        copies.wait((e, 1))
        for v in range(vecs):
            value = None
            for k in range(terms):
                term = jnp.dot(trans[v][k * width : (k + 1) * width], right_v[e, k], preferred_element_type=F32)
                value = term if value is None else value + term
            total[v] = jnp.where(alive, value, 0.0)
        for o in range(nop):
            start = pl.multiple_of((mine ^ o) * rows, rows)
            part = total[:, pl.ds(start, rows), :]
            if o % 2:
                send[o // 2, e] = part.astype(BF16)
            else:
                keep[o // 2, e] = part


def local(psi, left_env, right_env, sector_dims, right_place):
    nsec, nop = lax.axis_size("sec"), lax.axis_size("op")
    nb, vecs, width, _ = psi.shape
    terms = left_env.shape[0]
    rows = width // nop
    away = nsec - 1
    params = pltpu.CompilerParams(vmem_limit_bytes=40 * 2**20)
    shape = lambda *dims: jax.ShapeDtypeStruct(dims, BF16)
    dma = lambda *dims: pltpu.SemaphoreType.DMA(dims)

    def ship(x, axis, d):
        n = lax.axis_size(axis)
        return lax.ppermute(x, axis, [(i, i ^ d) for i in range(n)])

    def cost(flops, values):
        return pl.CostEstimate(flops=flops, bytes_accessed=2 * values, transcendentals=0)

    picked = pl.pallas_call(
        functools.partial(pick_kernel, nsec, nop, nb),
        in_specs=[SMEM, HBM, HBM],
        out_specs=[VMEM] * (2 * away),
        out_shape=[shape(vecs, rows, width)] * away + [shape(terms, width, width)] * away,
        scratch_shapes=[dma(2 * away)],
        compiler_params=pltpu.CompilerParams(vmem_limit_bytes=61 * 2**20),
        cost_estimate=cost(0, 0),
        name="pick",
    )(right_place, psi, left_env)
    pieces = [ship(picked[d - 1], "sec", d) for d in range(1, nsec)]
    lefts = {d: ship(picked[away + d - 1], "sec", d) for d in range(1, nsec)}

    def gather(pieces):
        stacked = pl.pallas_call(
            stack_kernel,
            in_specs=[ANY] * away,
            out_specs=VMEM,
            out_shape=shape(away, vecs, rows, width),
            scratch_shapes=[dma(away)],
            compiler_params=params,
            cost_estimate=cost(LONG, 0),
            name="stack",
        )(*pieces)
        gathered = {0: stacked}
        bit = nop // 2
        while bit:
            for o in sorted(gathered):
                gathered[o ^ bit] = ship(gathered[o], "op", bit)
            bit //= 2
        return [gathered[o] for o in range(nop)]

    def group(rounds, gathered, lefts, after):
        count = len(rounds)
        given = list(after) + (list(gathered) + [lefts[d] for d in rounds if d] if any(rounds) else [])
        value, send = pl.pallas_call(
            functools.partial(work_kernel, rounds, len(after), nsec, nop, nb),
            in_specs=[SMEM, SMEM, HBM, HBM, HBM] + [ANY] * len(given),
            out_specs=[VMEM] * 2,
            out_shape=[
                jax.ShapeDtypeStruct((nop // 2, count, vecs, rows, width), F32),
                shape(nop // 2, count, vecs, rows, width),
            ],
            scratch_shapes=[
                pltpu.VMEM((count, vecs, width, width), BF16),
                pltpu.VMEM((count, terms, width, width), BF16),
                pltpu.VMEM((count, terms, width, width), BF16),
                pltpu.VMEM((vecs, width, width), F32),
                dma(count * (nop + 2)),
            ],
            compiler_params=params,
            cost_estimate=cost(0, 0),
            name="work",
        )(right_place, sector_dims, psi, left_env, right_env, *given)
        bit = 1
        while True:
            value = value + ship(send, "op", bit).astype(F32)
            bit *= 2
            if bit == nop:
                break
            value, send = value[0::2], value[1::2].astype(BF16)
        return list(value[0].astype(BF16))

    def region(fn, *operands):
        like = jax.eval_shape(fn, *operands)
        none = lambda *operands: jax.tree.map(lambda x: jnp.zeros(x.shape, x.dtype), like)
        return lax.cond(right_place[0] >= 0, fn, none, *operands)

    gathered = gather(pieces)
    half = nsec // 2 + 1
    groups = [([0, 1], True, []), (list(range(2, half)), False, [0]), (list(range(half, nsec)), False, [0])]
    ready = {}
    for rounds, apart, waits in groups:
        arrived = {d: lefts[d] for d in rounds if d}
        after = [ready[d] for d in waits]
        if apart:
            values = region(functools.partial(group, rounds), gathered, arrived, after)
        else:
            values = group(rounds, gathered, arrived, after)
        for d, value in zip(rounds, values):
            ready[d] = value

    slots = lax.axis_index("sec") * nb + jnp.arange(nb, dtype=jnp.int32)
    blocks = jnp.arange(right_place.shape[0], dtype=jnp.int32)
    block = jnp.sum(jnp.where(right_place[None, :] == slots[:, None], blocks[None, :], 0), axis=1)
    round_of = (block // nb) ^ lax.axis_index("sec")
    sigma = ready[0][None]
    for d in range(1, nsec):
        sigma = jnp.where((round_of == d)[:, None, None, None], ready[d][None], sigma)
    return sigma


def solution(mesh):
    return jax.shard_map(
        local,
        mesh=mesh,
        in_specs=(
            P(("grp", "sec"), None, None, None),
            P("op", ("grp", "sec"), None, None),
            P("op", ("grp", "sec"), None, None),
            P(None, "grp"),
            P("grp"),
        ),
        out_specs=P(("grp", "sec"), None, "op", None),
        check_vma=False,
    )
```

```python
import functools

import jax
import jax.numpy as jnp
from jax import lax
from jax.experimental import pallas as pl
from jax.experimental.pallas import tpu as pltpu
from jax.sharding import PartitionSpec as P

ANY = pl.BlockSpec(memory_space=pl.ANY)
HBM = pl.BlockSpec(memory_space=pltpu.HBM)
SMEM = pl.BlockSpec(memory_space=pltpu.SMEM)
VMEM = pl.BlockSpec(memory_space=pltpu.VMEM)
F32 = jnp.float32
BF16 = jnp.bfloat16
EVERY = slice(None)


def find(place, nb, left, right):
    block, slot, found = jnp.int32(0), jnp.int32(0), jnp.bool_(False)
    for i in range(nb):
        at = place[left * nb + i]
        hit = lax.div(at, jnp.int32(nb)) == right
        block = jnp.where(hit, jnp.int32(i), block)
        slot = jnp.where(hit, lax.rem(at, jnp.int32(nb)), slot)
        found = found | hit
    return block, slot, found


def chunk(ref, lead, index, rows):
    return ref.at[(*lead, pl.ds(pl.multiple_of(index * rows, rows), rows))]


class Copies:
    def __init__(self, sems):
        self.sems, self.used, self.groups = sems, 0, {}

    def add(self, group, src, dst):
        copy = pltpu.make_async_copy(src, dst, self.sems.at[self.used])
        self.used += 1
        copy.start()
        self.groups.setdefault(group, []).append(copy)

    def wait(self, group):
        for copy in self.groups.pop(group):
            copy.wait()


def pick_kernel(nsec, nop, nb, place, psi, left_env, *rest):
    outs, copies = rest[:-1], Copies(rest[-1])
    me, mine = lax.axis_index("sec"), lax.axis_index("op")
    found = [find(place, nb, me, me ^ d)[0] for d in range(1, nsec)]
    for n, block in enumerate(found):
        copies.add(0, left_env.at[:, block], outs[nsec - 1 + n])
    for n, block in enumerate(found):
        copies.add(0, chunk(psi, (block, EVERY), mine, psi.shape[-2] // nop), outs[n])
    copies.wait(0)


def stack_kernel(*refs):
    pieces, out, copies = refs[:-2], refs[-2], Copies(refs[-1])
    for n, piece in enumerate(pieces):
        copies.add(0, piece, out.at[n])
    copies.wait(0)


def work_kernel(rounds, waits, nsec, nop, nb, place, dims, psi, left_env, right_env, *rest):
    count = len(rounds)
    far = [d for d in rounds if d]
    rest = rest[waits:]
    pieces, rest = (rest[:nop], rest[nop:]) if far else ((), rest)
    lefts, rest = rest[: len(far)], rest[len(far) :]
    keep, send, psi_v, left_v, right_v, total, sems = rest
    copies = Copies(sems)
    me, mine = lax.axis_index("sec"), lax.axis_index("op")
    terms, vecs, width = left_v.shape[1], psi_v.shape[1], psi_v.shape[-1]
    rows = width // nop
    found = [find(place, nb, me ^ d, me) for d in rounds]
    for e, d in enumerate(rounds):
        block, slot, _ = found[e]
        if d == 0:
            copies.add((e, 0), psi.at[block], psi_v.at[e])
            copies.add((e, 0), left_env.at[:, block], left_v.at[e])
        else:
            for o in range(nop):
                copies.add((e, 0), pieces[o].at[d - 1], chunk(psi_v, (e, EVERY), mine ^ o, rows))
            copies.add((e, 0), lefts[far.index(d)], left_v.at[e])
        copies.add((e, 1), right_env.at[:, slot], right_v.at[e])
    row = lax.broadcasted_iota(jnp.int32, (width, width), 0)
    col = lax.broadcasted_iota(jnp.int32, (width, width), 1)
    for e, d in enumerate(rounds):
        block, _, there = found[e]
        source = me ^ d
        live_rows = jnp.where(there, dims[0, source * nb + block], 0)
        live_cols = jnp.where(there, dims[1, source * nb + block], 0)
        alive = (row < live_rows) & (col < live_cols)
        copies.wait((e, 0))
        left = left_v[e].reshape(terms * width, width)
        trans = []
        for v in range(vecs):
            masked = jnp.where(alive, psi_v[e, v], jnp.zeros_like(psi_v[e, v]))
            trans.append(jnp.dot(left, masked, preferred_element_type=F32).astype(BF16))
        copies.wait((e, 1))
        for v in range(vecs):
            value = None
            for k in range(terms):
                term = jnp.dot(trans[v][k * width : (k + 1) * width], right_v[e, k], preferred_element_type=F32)
                value = term if value is None else value + term
            total[v] = jnp.where(alive, value, 0.0)
        for o in range(nop):
            start = pl.multiple_of((mine ^ o) * rows, rows)
            part = total[:, pl.ds(start, rows), :]
            if o % 2:
                send[o // 2, e] = part.astype(BF16)
            else:
                keep[o // 2, e] = part


def local(psi, left_env, right_env, sector_dims, right_place):
    nsec, nop = lax.axis_size("sec"), lax.axis_size("op")
    nb, vecs, width, _ = psi.shape
    terms = left_env.shape[0]
    rows = width // nop
    away = nsec - 1
    params = pltpu.CompilerParams(vmem_limit_bytes=40 * 2**20)
    shape = lambda *dims: jax.ShapeDtypeStruct(dims, BF16)
    dma = lambda *dims: pltpu.SemaphoreType.DMA(dims)

    def ship(x, axis, d):
        n = lax.axis_size(axis)
        return lax.ppermute(x, axis, [(i, i ^ d) for i in range(n)])

    def cost(flops, values):
        return pl.CostEstimate(flops=flops, bytes_accessed=2 * values, transcendentals=0)

    picked = pl.pallas_call(
        functools.partial(pick_kernel, nsec, nop, nb),
        in_specs=[SMEM, HBM, HBM],
        out_specs=[VMEM] * (2 * away),
        out_shape=[shape(vecs, rows, width)] * away + [shape(terms, width, width)] * away,
        scratch_shapes=[dma(2 * away)],
        compiler_params=pltpu.CompilerParams(vmem_limit_bytes=40 * 2**20),
        cost_estimate=cost(0, 0),
        name="pick",
    )(right_place, psi, left_env)
    pieces = [ship(picked[d - 1], "sec", d) for d in range(1, nsec)]
    lefts = {d: ship(picked[away + d - 1], "sec", d) for d in range(1, nsec)}

    def gather(pieces):
        stacked = pl.pallas_call(
            stack_kernel,
            in_specs=[ANY] * away,
            out_specs=VMEM,
            out_shape=shape(away, vecs, rows, width),
            scratch_shapes=[dma(away)],
            compiler_params=params,
            cost_estimate=cost(0, 0),
            name="stack",
        )(*pieces)
        gathered = {0: stacked}
        bit = nop // 2
        while bit:
            for o in sorted(gathered):
                gathered[o ^ bit] = ship(gathered[o], "op", bit)
            bit //= 2
        return [gathered[o] for o in range(nop)]

    def group(rounds, gathered, lefts, after):
        count = len(rounds)
        given = list(after) + (list(gathered) + [lefts[d] for d in rounds if d] if any(rounds) else [])
        value, send = pl.pallas_call(
            functools.partial(work_kernel, rounds, len(after), nsec, nop, nb),
            in_specs=[SMEM, SMEM, HBM, HBM, HBM] + [ANY] * len(given),
            out_specs=[VMEM] * 2,
            out_shape=[
                jax.ShapeDtypeStruct((nop // 2, count, vecs, rows, width), F32),
                shape(nop // 2, count, vecs, rows, width),
            ],
            scratch_shapes=[
                pltpu.VMEM((count, vecs, width, width), BF16),
                pltpu.VMEM((count, terms, width, width), BF16),
                pltpu.VMEM((count, terms, width, width), BF16),
                pltpu.VMEM((vecs, width, width), F32),
                dma(count * (nop + 2)),
            ],
            compiler_params=params,
            cost_estimate=cost(0, 0),
            name="work",
        )(right_place, sector_dims, psi, left_env, right_env, *given)
        bit = 1
        while True:
            value = value + ship(send, "op", bit).astype(F32)
            bit *= 2
            if bit == nop:
                break
            value, send = value[0::2], value[1::2].astype(BF16)
        return list(value[0].astype(BF16))

    def region(fn, *operands):
        like = jax.eval_shape(fn, *operands)
        none = lambda *operands: jax.tree.map(lambda x: jnp.zeros(x.shape, x.dtype), like)
        return lax.cond(right_place[0] >= 0, fn, none, *operands)

    gathered = gather(pieces)
    half = nsec // 2 + 1
    groups = [([1], True, []), (list(range(2, half)), False, [1]), ([0, *range(half, nsec)], False, [1])]
    ready = {}
    for rounds, apart, waits in groups:
        arrived = {d: lefts[d] for d in rounds if d}
        after = [ready[d] for d in waits]
        if apart:
            values = region(functools.partial(group, rounds), gathered, arrived, after)
        else:
            values = group(rounds, gathered, arrived, after)
        for d, value in zip(rounds, values):
            ready[d] = value

    slots = lax.axis_index("sec") * nb + jnp.arange(nb, dtype=jnp.int32)
    blocks = jnp.arange(right_place.shape[0], dtype=jnp.int32)
    block = jnp.sum(jnp.where(right_place[None, :] == slots[:, None], blocks[None, :], 0), axis=1)
    round_of = (block // nb) ^ lax.axis_index("sec")
    sigma = ready[0][None]
    for d in range(1, nsec):
        sigma = jnp.where((round_of == d)[:, None, None, None], ready[d][None], sigma)
    return sigma


def solution(mesh):
    return jax.shard_map(
        local,
        mesh=mesh,
        in_specs=(
            P(("grp", "sec"), None, None, None),
            P("op", ("grp", "sec"), None, None),
            P("op", ("grp", "sec"), None, None),
            P(None, "grp"),
            P("grp"),
        ),
        out_specs=P(("grp", "sec"), None, "op", None),
        check_vma=False,
    )
```

```python
import functools

import jax
import jax.numpy as jnp
from jax import lax
from jax.experimental import pallas as pl
from jax.experimental.pallas import tpu as pltpu
from jax.sharding import PartitionSpec as P

ANY = pl.BlockSpec(memory_space=pl.ANY)
HBM = pl.BlockSpec(memory_space=pltpu.HBM)
SMEM = pl.BlockSpec(memory_space=pltpu.SMEM)
VMEM = pl.BlockSpec(memory_space=pltpu.VMEM)
F32 = jnp.float32
BF16 = jnp.bfloat16
EVERY = slice(None)


def find(place, nb, left, right):
    block, slot, found = jnp.int32(0), jnp.int32(0), jnp.bool_(False)
    for i in range(nb):
        at = place[left * nb + i]
        hit = lax.div(at, jnp.int32(nb)) == right
        block = jnp.where(hit, jnp.int32(i), block)
        slot = jnp.where(hit, lax.rem(at, jnp.int32(nb)), slot)
        found = found | hit
    return block, slot, found


def chunk(ref, lead, index, rows):
    return ref.at[(*lead, pl.ds(pl.multiple_of(index * rows, rows), rows))]


class Copies:
    def __init__(self, sems):
        self.sems, self.used, self.groups = sems, 0, {}

    def add(self, group, src, dst):
        copy = pltpu.make_async_copy(src, dst, self.sems.at[self.used])
        self.used += 1
        copy.start()
        self.groups.setdefault(group, []).append(copy)

    def wait(self, group):
        for copy in self.groups.pop(group):
            copy.wait()


def pick_kernel(nsec, nop, nb, place, psi, left_env, *rest):
    outs, copies = rest[:-1], Copies(rest[-1])
    me, mine = lax.axis_index("sec"), lax.axis_index("op")
    found = [find(place, nb, me, me ^ d)[0] for d in range(1, nsec)]
    for n, block in enumerate(found):
        copies.add(0, left_env.at[:, block], outs[nsec - 1 + n])
    for n, block in enumerate(found):
        copies.add(0, chunk(psi, (block, EVERY), mine, psi.shape[-2] // nop), outs[n])
    copies.wait(0)


def keep_kernel(nsec, nb, place, right_env, after, rights, sems):
    copies = Copies(sems)
    me = lax.axis_index("sec")
    for d in range(nsec):
        _, slot, _ = find(place, nb, me ^ d, me)
        copies.add(0, right_env.at[:, slot], rights.at[d])
    copies.wait(0)


def stack_kernel(after, *refs):
    pieces, out, copies = refs[:-2], refs[-2], Copies(refs[-1])
    for n, piece in enumerate(pieces):
        copies.add(0, piece, out.at[n])
    copies.wait(0)


def work_kernel(rounds, waits, nsec, nop, nb, place, dims, psi, left_env, rights, *rest):
    count = len(rounds)
    far = [d for d in rounds if d]
    rest = rest[waits:]
    pieces, rest = (rest[:nop], rest[nop:]) if far else ((), rest)
    lefts, rest = rest[: len(far)], rest[len(far) :]
    keep, send, psi_v, left_v, right_v, total, sems = rest
    copies = Copies(sems)
    me, mine = lax.axis_index("sec"), lax.axis_index("op")
    terms, vecs, width = left_v.shape[1], psi_v.shape[1], psi_v.shape[-1]
    rows = width // nop
    found = [find(place, nb, me ^ d, me) for d in rounds]
    for e, d in enumerate(rounds):
        block, _, _ = found[e]
        if d == 0:
            copies.add((e, 0), psi.at[block], psi_v.at[e])
            copies.add((e, 0), left_env.at[:, block], left_v.at[e])
        else:
            for o in range(nop):
                copies.add((e, 0), pieces[o].at[d - 1], chunk(psi_v, (e, EVERY), mine ^ o, rows))
            copies.add((e, 0), lefts[far.index(d)], left_v.at[e])
        copies.add((e, 1), rights.at[d], right_v.at[e])
    row = lax.broadcasted_iota(jnp.int32, (width, width), 0)
    col = lax.broadcasted_iota(jnp.int32, (width, width), 1)
    for e, d in enumerate(rounds):
        block, _, there = found[e]
        source = me ^ d
        live_rows = jnp.where(there, dims[0, source * nb + block], 0)
        live_cols = jnp.where(there, dims[1, source * nb + block], 0)
        alive = (row < live_rows) & (col < live_cols)
        copies.wait((e, 0))
        left = left_v[e].reshape(terms * width, width)
        trans = []
        for v in range(vecs):
            masked = jnp.where(alive, psi_v[e, v], jnp.zeros_like(psi_v[e, v]))
            trans.append(jnp.dot(left, masked, preferred_element_type=F32).astype(BF16))
        copies.wait((e, 1))
        for v in range(vecs):
            value = None
            for k in range(terms):
                term = jnp.dot(trans[v][k * width : (k + 1) * width], right_v[e, k], preferred_element_type=F32)
                value = term if value is None else value + term
            total[v] = jnp.where(alive, value, 0.0)
        for o in range(nop):
            start = pl.multiple_of((mine ^ o) * rows, rows)
            part = total[:, pl.ds(start, rows), :]
            if o % 2:
                send[o // 2, e] = part.astype(BF16)
            else:
                keep[o // 2, e] = part


def local(psi, left_env, right_env, sector_dims, right_place):
    nsec, nop = lax.axis_size("sec"), lax.axis_size("op")
    nb, vecs, width, _ = psi.shape
    terms = left_env.shape[0]
    rows = width // nop
    away = nsec - 1
    params = pltpu.CompilerParams(vmem_limit_bytes=40 * 2**20)
    shape = lambda *dims: jax.ShapeDtypeStruct(dims, BF16)
    dma = lambda *dims: pltpu.SemaphoreType.DMA(dims)

    def ship(x, axis, d):
        n = lax.axis_size(axis)
        return lax.ppermute(x, axis, [(i, i ^ d) for i in range(n)])

    def cost(flops, values):
        return pl.CostEstimate(flops=flops, bytes_accessed=2 * values, transcendentals=0)

    picked = pl.pallas_call(
        functools.partial(pick_kernel, nsec, nop, nb),
        in_specs=[SMEM, HBM, HBM],
        out_specs=[VMEM] * (2 * away),
        out_shape=[shape(vecs, rows, width)] * away + [shape(terms, width, width)] * away,
        scratch_shapes=[dma(2 * away)],
        compiler_params=pltpu.CompilerParams(vmem_limit_bytes=40 * 2**20),
        cost_estimate=cost(0, 0),
        name="pick",
    )(right_place, psi, left_env)
    pieces = [ship(picked[d - 1], "sec", d) for d in range(1, nsec)]
    lefts = {d: ship(picked[away + d - 1], "sec", d) for d in range(1, nsec)}

    rights = pl.pallas_call(
        functools.partial(keep_kernel, nsec, nb),
        in_specs=[SMEM, HBM, ANY],
        out_specs=VMEM,
        out_shape=shape(nsec, terms, width, width),
        scratch_shapes=[dma(nsec)],
        compiler_params=pltpu.CompilerParams(vmem_limit_bytes=40 * 2**20),
        cost_estimate=cost(0, 0),
        name="keep",
    )(right_place, right_env, picked[0])

    def gather(pieces):
        stacked = pl.pallas_call(
            stack_kernel,
            in_specs=[ANY] * nsec,
            out_specs=VMEM,
            out_shape=shape(away, vecs, rows, width),
            scratch_shapes=[dma(away)],
            compiler_params=params,
            cost_estimate=cost(0, 0),
            name="stack",
        )(rights, *pieces)
        gathered = {0: stacked}
        bit = nop // 2
        while bit:
            for o in sorted(gathered):
                gathered[o ^ bit] = ship(gathered[o], "op", bit)
            bit //= 2
        return [gathered[o] for o in range(nop)]

    def group(rounds, gathered, lefts, after):
        count = len(rounds)
        given = list(after) + (list(gathered) + [lefts[d] for d in rounds if d] if any(rounds) else [])
        value, send = pl.pallas_call(
            functools.partial(work_kernel, rounds, len(after), nsec, nop, nb),
            in_specs=[SMEM, SMEM, HBM, HBM, ANY] + [ANY] * len(given),
            out_specs=[VMEM] * 2,
            out_shape=[
                jax.ShapeDtypeStruct((nop // 2, count, vecs, rows, width), F32),
                shape(nop // 2, count, vecs, rows, width),
            ],
            scratch_shapes=[
                pltpu.VMEM((count, vecs, width, width), BF16),
                pltpu.VMEM((count, terms, width, width), BF16),
                pltpu.VMEM((count, terms, width, width), BF16),
                pltpu.VMEM((vecs, width, width), F32),
                dma(count * (nop + 2)),
            ],
            compiler_params=params,
            cost_estimate=cost(0, 0),
            name="work",
        )(right_place, sector_dims, psi, left_env, rights, *given)
        bit = 1
        while True:
            value = value + ship(send, "op", bit).astype(F32)
            bit *= 2
            if bit == nop:
                break
            value, send = value[0::2], value[1::2].astype(BF16)
        return list(value[0].astype(BF16))

    def region(fn, *operands):
        like = jax.eval_shape(fn, *operands)
        none = lambda *operands: jax.tree.map(lambda x: jnp.zeros(x.shape, x.dtype), like)
        return lax.cond(right_place[0] >= 0, fn, none, *operands)

    gathered = gather(pieces)
    half = nsec // 2 + 1
    groups = [([1], True, []), (list(range(2, half)), False, [1]), ([0, *range(half, nsec)], False, [1])]
    ready = {}
    for rounds, apart, waits in groups:
        arrived = {d: lefts[d] for d in rounds if d}
        after = [ready[d] for d in waits]
        if apart:
            values = region(functools.partial(group, rounds), gathered, arrived, after)
        else:
            values = group(rounds, gathered, arrived, after)
        for d, value in zip(rounds, values):
            ready[d] = value

    slots = lax.axis_index("sec") * nb + jnp.arange(nb, dtype=jnp.int32)
    blocks = jnp.arange(right_place.shape[0], dtype=jnp.int32)
    block = jnp.sum(jnp.where(right_place[None, :] == slots[:, None], blocks[None, :], 0), axis=1)
    round_of = (block // nb) ^ lax.axis_index("sec")
    sigma = ready[0][None]
    for d in range(1, nsec):
        sigma = jnp.where((round_of == d)[:, None, None, None], ready[d][None], sigma)
    return sigma


def solution(mesh):
    return jax.shard_map(
        local,
        mesh=mesh,
        in_specs=(
            P(("grp", "sec"), None, None, None),
            P("op", ("grp", "sec"), None, None),
            P("op", ("grp", "sec"), None, None),
            P(None, "grp"),
            P("grp"),
        ),
        out_specs=P(("grp", "sec"), None, "op", None),
        check_vma=False,
    )
```
